32 devices in a mesh: sh: 4 (over z), sw: 4 (over y, core), tp: 2 (over x).
Axes of the slice: x: 2, y: 2, z: 4, core: 2. Of those that a mesh axis runs over, the one named last changes fastest.
Arguments:
- queries: bfloat16 [2, 32, 32, 1536], P('tp', 'sh', 'sw'), may hold values from -6 to 6
- keys: bfloat16 [2, 32, 32, 1536], P('tp', 'sh', 'sw'), may hold values from -6 to 6
- values: bfloat16 [2, 32, 32, 1536], P('tp', 'sh', 'sw'), may hold values from -6 to 6
- attn_out: bfloat16 [2, 32, 32, 1536], P('tp', 'sh', 'sw'), may hold values from -6 to 6
- attn_grad: bfloat16 [2, 32, 32, 1536], P('tp', 'sh', 'sw'), may hold values from -192 to 192
- log_sum: float32 [2, 32, 32, 12], P('tp', 'sh', 'sw'), may hold values from 6.1 to 6.9
- window_dirs: int32 [12, 4], replicated, may hold values from 0 to 7, as said below
Outputs:
- q_grad: bfloat16 [2, 32, 32, 1536], P('tp', 'sh', 'sw')
- k_grad: bfloat16 [2, 32, 32, 1536], P('tp', 'sh', 'sw')
- v_grad: bfloat16 [2, 32, 32, 1536], P('tp', 'sh', 'sw')
The draws below stay inside these ranges and needn't reach their ends.
Inputs may be any that keep to these rules, and one draw needn't show every extreme that they name: `window_dirs`: each row names 4 different directions. Within each run of 6 consecutive heads (those of one index of tp) every direction is named by exactly half of the rows.
All inputs are finite; a program needn't handle non-finite values.
Results may differ from the reference program's by a relative error of at most 0.0056.
Values may be sent and summed in bfloat16 or wider, within the bound.
A program may use at most 64 MiB of HBM per device.

```python
import jax
import jax.numpy as jnp
from jax import lax

FRAMES = 2
TILE_H = 8
TILE_W = 8
HD = 128
HEADS_DEV = 6
HEADS = 12
HEIGHT = 32
WIDTH = 32
COLS = 1536
N_SH = 4
N_SW = 4


def draw_window_dirs(key, part):
    slot_ids = jnp.arange(4 * HEADS_DEV, dtype=jnp.int32)
    base_dirs = ((slot_ids + slot_ids // 8) % 8).reshape(HEADS_DEV, 4)
    groups = []
    for group_id in range(HEADS // HEADS_DEV):
        dir_order = jax.random.permutation(jax.random.fold_in(key, 2 * group_id), 8).astype(jnp.int32)
        head_order = jax.random.permutation(jax.random.fold_in(key, 2 * group_id + 1), HEADS_DEV).astype(jnp.int32)
        groups.append(dir_order[base_dirs][head_order])
    return jnp.concatenate(groups, axis=0).astype(jnp.int32)


def level_of(stream_key, shape, pieces, least, largest):
    def one(dim, parts):
        heights = jax.random.uniform(jax.random.fold_in(jax.random.fold_in(stream_key, 6), dim), (parts,), jnp.float32, least / len(pieces), largest / len(pieces))
        return jnp.repeat(jnp.exp(heights), shape[dim] // parts).reshape((-1,) + (1,) * (len(shape) - dim - 1))

    level = one(*pieces[0])
    for cut in pieces[1:]:
        level = level * one(*cut)
    return level


def noise(rng, extent, width, limit, shards=(), held_as=jnp.bfloat16):
    values = width * jax.random.normal(rng, extent, jnp.float32)
    if shards:
        values = values * level_of(rng, extent, shards, -0.22, 0.18)
    return jnp.clip(values, -limit, limit).astype(held_as)


def setup_inputs(seed: int = 0) -> dict:
    seeds = jax.random.split(jax.random.key(seed), 8)
    return {
        "queries": noise(seeds[0], (FRAMES, HEIGHT, WIDTH, COLS), 1.0, 6.0, ((0, 2), (1, 4), (2, 4))),
        "keys": noise(seeds[1], (FRAMES, HEIGHT, WIDTH, COLS), 1.0, 6.0, ((0, 2), (1, 4), (2, 4))),
        "values": noise(seeds[2], (FRAMES, HEIGHT, WIDTH, COLS), 1.0, 6.0, ((0, 2), (1, 4), (2, 4))),
        "attn_out": noise(seeds[3], (FRAMES, HEIGHT, WIDTH, COLS), 1.0, 6.0, ((0, 2), (1, 4), (2, 4))),
        "attn_grad": noise(seeds[4], (FRAMES, HEIGHT, WIDTH, COLS), 32.0, 192.0, ((0, 2), (1, 4), (2, 4))),
        "log_sum": jnp.clip(6.1 + 0.8000002 * jax.random.uniform(seeds[5], (FRAMES, HEIGHT, WIDTH, HEADS), jnp.float32) ** level_of(seeds[5], (FRAMES, HEIGHT, WIDTH, HEADS), ((0, 2), (1, 4), (2, 4)), -0.2, 0.2), 6.1, 6.9),
        "window_dirs": draw_window_dirs(jax.random.fold_in(seeds[7], 71), 0),
    }


NEIGHBOURS = ((-1, -1), (-1, 0), (-1, 1), (0, -1), (0, 1), (1, -1), (1, 0), (1, 1))


def rounded(array):
    return lax.optimization_barrier(array.astype(jnp.bfloat16)).astype(jnp.float32)


def reference(queries, keys, values, attn_out, attn_grad, log_sum, window_dirs):
    tile_tok = FRAMES * TILE_H * TILE_W
    score_scale = HD ** -0.5
    row_delta = jnp.sum((attn_grad.astype(jnp.float32) * attn_out.astype(jnp.float32)).reshape(FRAMES, HEIGHT, WIDTH, HEADS, HD), axis=4)

    def head_view(array):
        return array.reshape(FRAMES, N_SH, TILE_H, N_SW, TILE_W, HEADS, HD)

    def stat_view(array):
        return array.reshape(FRAMES, N_SH, TILE_H, N_SW, TILE_W, HEADS)

    q_view = head_view(queries)
    k_view = head_view(keys)
    v_view = head_view(values)
    g_view = head_view(attn_grad)
    lse_view = stat_view(log_sum)
    delta_view = stat_view(row_delta)
    offsets = jnp.array(NEIGHBOURS, dtype=jnp.int32)
    row_steps = offsets[window_dirs, 0]
    col_steps = offsets[window_dirs, 1]
    head_ids = jnp.broadcast_to(jnp.arange(HEADS, dtype=jnp.int32)[:, None], (HEADS, 4))
    ones_col = jnp.ones((HEADS, 1), jnp.float32)

    def own_heads(view, grid_row, grid_col):
        return view[:, grid_row, :, grid_col].reshape(tile_tok, HEADS, HD).astype(jnp.float32)

    def own_stats(view, grid_row, grid_col):
        return view[:, grid_row, :, grid_col].reshape(tile_tok, HEADS).T

    def near_heads(view, rows_at, cols_at):
        return view[:, rows_at, :, cols_at, :, head_ids].reshape(HEADS, 4, tile_tok, HD).astype(jnp.float32)

    def near_stats(view, rows_at, cols_at):
        return view[:, rows_at, :, cols_at, :, head_ids].reshape(HEADS, 4, tile_tok)

    def placed(rows_raw, cols_raw):
        live = (rows_raw >= 0) & (rows_raw < N_SH) & (cols_raw >= 0) & (cols_raw < N_SW)
        return jnp.clip(rows_raw, 0, N_SH - 1), jnp.clip(cols_raw, 0, N_SW - 1), live.astype(jnp.float32)

    def one_tile(tile_index):
        grid_row = tile_index // N_SW
        grid_col = tile_index % N_SW
        q_here = own_heads(q_view, grid_row, grid_col)
        k_here = own_heads(k_view, grid_row, grid_col)
        v_here = own_heads(v_view, grid_row, grid_col)
        g_here = own_heads(g_view, grid_row, grid_col)
        lse_here = own_stats(lse_view, grid_row, grid_col)
        delta_here = own_stats(delta_view, grid_row, grid_col)
        near_row, near_col, live_near = placed(grid_row + row_steps, grid_col + col_steps)
        k_all = jnp.concatenate([jnp.transpose(k_here, (1, 0, 2))[:, None], near_heads(k_view, near_row, near_col)], axis=1)
        v_all = jnp.concatenate([jnp.transpose(v_here, (1, 0, 2))[:, None], near_heads(v_view, near_row, near_col)], axis=1)
        live_all = jnp.concatenate([ones_col, live_near], axis=1)
        scores = score_scale * jnp.einsum("thd,hjsd->htjs", q_here, k_all)
        attn_prob = jnp.exp(scores - lse_here[:, :, None, None]) * live_all[:, None, :, None]
        grad_prob = jnp.einsum("thd,hjsd->htjs", g_here, v_all)
        grad_score = attn_prob * (grad_prob - delta_here[:, :, None, None])
        score_bf = rounded(grad_score)
        q_grad = score_scale * jnp.einsum("htjs,hjsd->thd", score_bf, k_all)
        k_self = score_scale * jnp.einsum("hts,thd->hsd", score_bf[:, :, 0], q_here)
        v_self = jnp.einsum("hts,thd->hsd", rounded(attn_prob[:, :, 0]), g_here)
        far_row, far_col, live_far = placed(grid_row - row_steps, grid_col - col_steps)
        q_far = near_heads(q_view, far_row, far_col)
        g_far = near_heads(g_view, far_row, far_col)
        lse_far = near_stats(lse_view, far_row, far_col)
        delta_far = near_stats(delta_view, far_row, far_col)
        scores_far = score_scale * jnp.einsum("hjtd,shd->hjts", q_far, k_here)
        prob_far = jnp.exp(scores_far - lse_far[:, :, :, None]) * live_far[:, :, None, None]
        grad_far = jnp.einsum("hjtd,shd->hjts", g_far, v_here)
        score_far = prob_far * (grad_far - delta_far[:, :, :, None])
        k_pieces = score_scale * jnp.einsum("hjts,hjtd->hjsd", rounded(score_far), q_far)
        v_pieces = jnp.einsum("hjts,hjtd->hjsd", rounded(prob_far), g_far)
        k_total = k_self + jnp.sum(rounded(k_pieces), axis=1)
        v_total = v_self + jnp.sum(rounded(v_pieces), axis=1)
        q_out = q_grad.astype(jnp.bfloat16).reshape(tile_tok, HEADS * HD)
        k_out = jnp.transpose(k_total, (1, 0, 2)).astype(jnp.bfloat16).reshape(tile_tok, HEADS * HD)
        v_out = jnp.transpose(v_total, (1, 0, 2)).astype(jnp.bfloat16).reshape(tile_tok, HEADS * HD)
        return q_out, k_out, v_out

    q_tiles, k_tiles, v_tiles = lax.map(one_tile, jnp.arange(N_SH * N_SW, dtype=jnp.int32))

    def from_tiles(tiles):
        shaped = tiles.reshape(N_SH, N_SW, FRAMES, TILE_H, TILE_W, HEADS * HD)
        return jnp.transpose(shaped, (2, 0, 3, 1, 4, 5)).reshape(FRAMES, HEIGHT, WIDTH, HEADS * HD)

    return (from_tiles(q_tiles), from_tiles(k_tiles), from_tiles(v_tiles))
```

```python
import functools

import jax
import jax.numpy as jnp
from jax import lax
from jax.experimental import pallas as pl
from jax.experimental.pallas import tpu as pltpu
from jax.sharding import PartitionSpec as P

E_OF = (1, 7, 4, 0, 3, 2, 8, 5)
BF = jnp.bfloat16
F32 = jnp.float32
NT = (((1,), (1,)), ((), ()))
TN = (((0,), (0,)), ((), ()))


def kernel(
    n_sh, n_sw, half, hd,
    q_ref, k_ref, v_ref, g_ref, o_ref, lse_ref, wd_ref,
    dq_out, dk_out, dv_out,
    zb00, zb01, zb10, zb11, kv0, kv1, qg, pieces, packed, stats,
    rs00, rs01, rs02, rs10, rs11, rs12, dqs, dkp, own_kv, own_q,
    zsend, zback, xsend, xback, head_of, rank_of, member_of, flat_of,
    zs, zr, zts, ztr, xs, xr, ws, wr, wts, wtr, rs, rr, rzs, rzr, rxs, rxr,
):
    row = lax.axis_index("sh")
    col = lax.axis_index("sw")
    part = lax.axis_index("tp")
    zb = ((zb00, zb01), (zb10, zb11))
    kv = (kv0, kv1)
    rsw = ((rs00, rs01, rs02), (rs10, rs11, rs12))
    third = half // 2
    tok = q_ref.shape[0]
    scale = hd ** -0.5
    row_ok = lambda step: (row + step >= 0) & (row + step < n_sh)
    col_ok = lambda step: (col + step >= 0) & (col + step < n_sw)
    row_step = (0, -1, 1)
    col_step = (-1, 1)

    def remote(src, dst, ssem, rsem, device):
        return pltpu.make_async_remote_copy(
            src_ref=src, dst_ref=dst, send_sem=ssem, recv_sem=rsem,
            device_id=device, device_id_type=pl.DeviceIdType.MESH,
        )

    def copy_z(run, i):
        return remote(qg.at[run], zb[run][i], zs.at[run, i], zr.at[run, i], {"sh": row + 2 * i - 1})

    def copy_zstat(i):
        return remote(stats.at[6], stats.at[7 + i], zts.at[i], ztr.at[i], {"sh": row + 2 * i - 1})

    def copy_x(run):
        src = kv[run].at[:, :, pl.ds(0, tok)]
        dst = kv[run].at[:, :, pl.ds(tok, tok)]
        return remote(src, dst, xs.at[run], xr.at[run], {"tp": 1 - part})

    def copy_w(run, c, i):
        e = c * 3 + i
        return remote(packed.at[run, e], pieces.at[run, e], ws.at[run, e], wr.at[run, e], {"sw": col + col_step[c]})

    def copy_wstat(c, i):
        e = c * 3 + i
        return remote(stats.at[6 + i], stats.at[e], wts.at[e], wtr.at[e], {"sw": col + col_step[c]})

    def copy_back(run, c, i):
        e = c * 3 + i
        return remote(dqs.at[run * 9 + e], rsw[run][i].at[c], rs.at[run, e], rr.at[run, e], {"sw": col - col_step[c]})

    def copy_zback(run, i):
        return remote(zsend.at[run, i], zback.at[run, i], rzs.at[run, i], rzr.at[run, i], {"sh": row - (2 * i - 1)})

    def copy_xback(run):
        return remote(xsend.at[run], xback.at[run], rxs.at[run], rxr.at[run], {"tp": 1 - part})

    barrier = pltpu.get_barrier_semaphore()
    pl.semaphore_signal(barrier, inc=1, device_id={"tp": 1 - part}, device_id_type=pl.DeviceIdType.MESH)
    for step in (-1, 1):
        @pl.when(row_ok(step))
        def _():
            pl.semaphore_signal(barrier, inc=1, device_id={"sh": row + step}, device_id_type=pl.DeviceIdType.MESH)

        @pl.when(col_ok(step))
        def _():
            pl.semaphore_signal(barrier, inc=1, device_id={"sw": col + step}, device_id_type=pl.DeviceIdType.MESH)
    for run in (0, 1):
        for h in range(half):
            cols = slice((run * half + h) * hd, (run * half + h + 1) * hd)
            qg[run, 0, h] = q_ref[:, cols]
            qg[run, 1, h] = g_ref[:, cols]
            kv[run][0, h, :tok] = k_ref[:, cols]
            kv[run][1, h, :tok] = v_ref[:, cols]
    count = 1
    for step in (-1, 1):
        count = count + row_ok(step).astype(jnp.int32) + col_ok(step).astype(jnp.int32)
    pl.semaphore_wait(barrier, count)

    for run in (0, 1):
        for i in (0, 1):
            @pl.when(row_ok(2 * i - 1))
            def _():
                copy_z(run, i).start()
        copy_x(run).start()

    for run in (0, 1):
        dirs = [[wd_ref[run * half + h, j] for j in range(4)] for h in range(half)]
        flat = [[jnp.int32(0) for j in range(4)] for h in range(half)]
        for d in range(8):
            e = E_OF[d]
            seen = jnp.int32(0)
            heads = [jnp.int32(0) for _ in range(third)]
            for h in range(half):
                named = [(dirs[h][j] == d).astype(jnp.int32) for j in range(4)]
                member = named[0] + named[1] + named[2] + named[3]
                rank = jnp.minimum(seen, third - 1)
                rank_of[(run * 9 + e) * half + h] = rank
                member_of[(run * 9 + e) * half + h] = member
                at = (run * 9 + e) * third + rank
                for j in range(4):
                    flat[h][j] = flat[h][j] + named[j] * at
                for s in range(third):
                    heads[s] = heads[s] + member * (seen == s).astype(jnp.int32) * h
                seen = seen + member
            for s in range(third):
                head_of[(run * 9 + e) * third + s] = heads[s]
        for h in range(half):
            for j in range(4):
                flat_of[(run * half + h) * 4 + j] = flat[h][j]

    def pack(run, c, i):
        e = c * 3 + i
        for s in range(third):
            h = head_of[(run * 9 + e) * third + s]
            for a in (0, 1):
                block = qg[run, a, h] if i == 0 else zb[run][i - 1][a, h]
                if c == 2:
                    pieces[run, e, s, a] = block
                else:
                    packed[run, e, s, a] = block

    for run in (0, 1):
        for c in (0, 1):
            @pl.when(col_ok(col_step[c]))
            def _():
                pack(run, c, 0)
                copy_w(run, c, 0).start()

    lane = lax.broadcasted_iota(jnp.int32, (tok, hd), 1)
    table = jnp.zeros((tok, hd), F32)
    for run in (0, 1):
        for h in range(half):
            at = run * half + h
            cols = slice(at * hd, (at + 1) * hd)
            delta = jnp.sum(g_ref[:, cols].astype(F32) * o_ref[:, cols].astype(F32), axis=1, keepdims=True)
            table = jnp.where(lane == run * 16 + h, lse_ref[:, at:at + 1], table)
            table = jnp.where(lane == run * 16 + 8 + h, delta, table)
    square = jnp.concatenate([table, jnp.zeros((hd - tok, hd), F32)], axis=0) if tok < hd else table
    stats[6] = square.T[:32, :]
    for i in (0, 1):
        @pl.when(row_ok(2 * i - 1))
        def _():
            copy_zstat(i).start()
    for c in (0, 1):
        @pl.when(col_ok(col_step[c]))
        def _():
            copy_wstat(c, 0).start()

    def clear(e, carry):
        i = lax.rem(e, 3)
        c = lax.div(e, 3)
        r_step = jnp.where(i == 0, 0, 2 * i - 3)
        c_step = jnp.where(c == 2, 0, 2 * c - 1)
        live = row_ok(-r_step) & col_ok(-c_step)

        @pl.when(jnp.logical_not(live))
        def _():
            for run in (0, 1):
                for s in range(third):
                    dkp[(run * 9 + e) * third + s] = jnp.zeros(dkp.shape[1:], BF)
        return carry

    lax.fori_loop(0, 9, clear, 0)
    for c in (0, 1):
        @pl.when(jnp.logical_not(col_ok(col_step[c])))
        def _():
            for run in (0, 1):
                for i in range(3):
                    rsw[run][i][c] = jnp.zeros(rs00.shape[1:], BF)
    for i in (0, 1):
        @pl.when(jnp.logical_not(row_ok(2 * i - 1)))
        def _():
            for run in (0, 1):
                zback[run, i] = jnp.zeros(zback.shape[2:], BF)

    sub = lax.broadcasted_iota(jnp.int32, (8, hd), 0)

    def one(run, h, q, g, stat):
        keys = kv[run][0, h]
        vals = kv[run][1, h]
        pick = sub == h
        lse = jnp.sum(jnp.where(pick, stat[run * 16:run * 16 + 8], 0.0), axis=0, keepdims=True)[:, :tok]
        delta = jnp.sum(jnp.where(pick, stat[run * 16 + 8:run * 16 + 16], 0.0), axis=0, keepdims=True)[:, :tok]
        scores = lax.dot_general(keys, q, NT, preferred_element_type=F32)
        prob = jnp.exp(scores * scale - lse)
        grad_prob = lax.dot_general(vals, g, NT, preferred_element_type=F32)
        score_bf = (prob * (grad_prob - delta)).astype(BF)
        prob_bf = prob.astype(BF)
        dv = jnp.dot(prob_bf, g, preferred_element_type=F32)
        dk = jnp.dot(score_bf, q, preferred_element_type=F32) * scale
        dq = lax.dot_general(score_bf, keys, TN, preferred_element_type=F32) * scale
        return dq, dk, dv

    def own(run):
        def body(t, carry):
            stat = stats[6]
            for u in range(3):
                h = t * 3 + u
                dq, dk, dv = one(run, h, qg[run, 0, h], qg[run, 1, h], stat)
                own_q[run * half + h] = dq
                own_kv[run * half + h, 0] = dk
                own_kv[run * half + h, 1] = dv
            return carry

        lax.fori_loop(0, half // 3, body, 0)

    def group(run, e):
        stat = stats[e]
        for s in range(third):
            h = head_of[(run * 9 + e) * third + s]
            dq, dk, dv = one(run, h, pieces[run, e, s, 0], pieces[run, e, s, 1], stat)
            dqs[run * 9 + e, s] = dq.astype(BF)
            dkp[(run * 9 + e) * third + s, 0] = dk.astype(BF)
            dkp[(run * 9 + e) * third + s, 1] = dv.astype(BF)

    def from_side(run, c, i):
        @pl.when(row_ok(-row_step[i]) & col_ok(-col_step[c]))
        def _():
            copy_w(run, c, i).wait_recv()
            if run == 0:
                copy_wstat(c, i).wait_recv()
            group(run, c * 3 + i)
            copy_back(run, c, i).start()

    def relay(run):
        for i in (1, 2):
            @pl.when(row_ok(-row_step[i]))
            def _():
                copy_z(run, i - 1).wait_recv()
                if run == 0:
                    copy_zstat(i - 1).wait_recv()
                for c in (0, 1):
                    @pl.when(col_ok(col_step[c]))
                    def _():
                        pack(run, c, i)
                        copy_w(run, c, i).start()
                        if run == 0:
                            copy_wstat(c, i).start()
                pack(run, 2, i)

    def from_rows(run):
        for i in (1, 2):
            @pl.when(row_ok(-row_step[i]))
            def _():
                group(run, 6 + i)

    def wait_back(run, i):
        for c in (0, 1):
            @pl.when(row_ok(-row_step[i]) & col_ok(col_step[c]))
            def _():
                copy_back(run, c, i).wait_recv()

    def gathered(run, i, h, total):
        for c in (0, 1, 2):
            if c == 2 and i == 0:
                continue
            e = c * 3 + i
            rank = rank_of[(run * 9 + e) * half + h]
            held = dqs[run * 9 + e, rank] if c == 2 else rsw[run][i][c, rank]
            block = held.astype(F32) * member_of[(run * 9 + e) * half + h].astype(F32)
            total = block if total is None else total + block
        return total

    def turn(run):
        for i in (1, 2):
            @pl.when(row_ok(-row_step[i]))
            def _():
                wait_back(run, i)

                def body(h, carry):
                    zsend[run, i - 1, h] = gathered(run, i, h, None).astype(BF)
                    return carry

                lax.fori_loop(0, half, body, 0)
                copy_zback(run, i - 1).start()

    def total_kv(run, h, rows, a):
        total = own_kv[run * half + h, a, rows]
        for j in range(4):
            at = flat_of[(run * half + h) * 4 + j]
            total = total + dkp[at, a, rows].astype(F32)
        return total

    def to_partner(run):
        def body(h, carry):
            for a in (0, 1):
                xsend[run, a, h] = total_kv(run, h, slice(tok, 2 * tok), a).astype(BF)
            return carry

        lax.fori_loop(0, half, body, 0)
        copy_xback(run).start()

    def finish_kv(run):
        copy_xback(run).wait_recv()

        def body(h, carry):
            cols = pl.ds(pl.multiple_of((run * half + h) * hd, hd), hd)
            for a, out in ((0, dk_out), (1, dv_out)):
                total = total_kv(run, h, slice(0, tok), a) + xback[run, a, h].astype(F32)
                out[:, cols] = total.astype(BF)
            return carry

        lax.fori_loop(0, half, body, 0)

    def finish_q(run):
        wait_back(run, 0)
        for i in (0, 1):
            @pl.when(row_ok(2 * i - 1))
            def _():
                copy_zback(run, i).wait_recv()

        def body(h, carry):
            cols = pl.ds(pl.multiple_of((run * half + h) * hd, hd), hd)
            total = gathered(run, 0, h, own_q[run * half + h])
            total = total + zback[run, 0, h].astype(F32) + zback[run, 1, h].astype(F32)
            dq_out[:, cols] = total.astype(BF)
            return carry

        lax.fori_loop(0, half, body, 0)

    copy_x(0).wait_recv()
    own(0)
    relay(0)
    from_rows(0)
    from_side(0, 0, 0)
    from_side(0, 1, 0)
    copy_x(1).wait_recv()
    relay(1)
    for c in (0, 1):
        for i in (1, 2):
            from_side(0, c, i)
    from_rows(1)
    to_partner(0)
    turn(0)
    own(1)
    from_side(1, 0, 0)
    from_side(1, 1, 0)
    for c in (0, 1):
        for i in (1, 2):
            from_side(1, c, i)
    to_partner(1)
    turn(1)
    finish_kv(0)
    finish_q(0)
    finish_kv(1)
    finish_q(1)

    for run in (0, 1):
        copy_x(run).wait_send()
        copy_xback(run).wait_send()
        for i in (0, 1):
            @pl.when(row_ok(2 * i - 1))
            def _():
                copy_z(run, i).wait_send()
                if run == 0:
                    copy_zstat(i).wait_send()

            @pl.when(row_ok(1 - 2 * i))
            def _():
                copy_zback(run, i).wait_send()
        for c in (0, 1):
            for i in range(3):
                @pl.when(row_ok(-row_step[i]) & col_ok(col_step[c]))
                def _():
                    copy_w(run, c, i).wait_send()
                    if run == 0:
                        copy_wstat(c, i).wait_send()

                @pl.when(row_ok(-row_step[i]) & col_ok(-col_step[c]))
                def _():
                    copy_back(run, c, i).wait_send()


def local(n_sh, n_sw, queries, keys, values, attn_out, attn_grad, log_sum, window_dirs):
    shape = queries.shape
    tok = shape[0] * shape[1] * shape[2]
    cols = shape[3]
    heads = log_sum.shape[3]
    half = heads // 2
    third = half // 2
    hd = cols // heads
    flat = lambda array: array.reshape(tok, array.shape[3])
    vmem = pl.BlockSpec(memory_space=pltpu.VMEM)
    smem = pl.BlockSpec(memory_space=pltpu.SMEM)
    dma = pltpu.SemaphoreType.DMA
    scratch = (
        [pltpu.VMEM((2, half, tok, hd), BF) for _ in range(4)]
        + [pltpu.VMEM((2, half, 2 * tok, hd), BF) for _ in range(2)]
        + [
            pltpu.VMEM((2, 2, half, tok, hd), BF),
            pltpu.VMEM((2, 9, third, 2, tok, hd), BF),
            pltpu.VMEM((2, 6, third, 2, tok, hd), BF),
            pltpu.VMEM((9, 32, hd), F32),
        ]
        + [pltpu.VMEM((2, third, tok, hd), BF) for _ in range(6)]
        + [
            pltpu.VMEM((18, third, tok, hd), BF),
            pltpu.VMEM((18 * third, 2, 2 * tok, hd), BF),
            pltpu.VMEM((heads, 2, 2 * tok, hd), F32),
            pltpu.VMEM((heads, tok, hd), F32),
            pltpu.VMEM((2, 2, half, tok, hd), BF),
            pltpu.VMEM((2, 2, half, tok, hd), BF),
            pltpu.VMEM((2, 2, half, tok, hd), BF),
            pltpu.VMEM((2, 2, half, tok, hd), BF),
            pltpu.SMEM((18 * third,), jnp.int32),
            pltpu.SMEM((18 * half,), jnp.int32),
            pltpu.SMEM((18 * half,), jnp.int32),
            pltpu.SMEM((heads * 4,), jnp.int32),
        ]
    )
    for sem in ((2, 2), (2,), (2,), (2, 6), (6,), (2, 6), (2, 2), (2,)):
        scratch += [dma(sem), dma(sem)]
    dq, dk, dv = pl.pallas_call(
        functools.partial(kernel, n_sh, n_sw, half, hd),
        out_shape=[jax.ShapeDtypeStruct((tok, cols), BF)] * 3,
        in_specs=[vmem] * 6 + [smem],
        out_specs=[vmem] * 3,
        scratch_shapes=scratch,
        compiler_params=pltpu.CompilerParams(
            collective_id=0, has_side_effects=True, vmem_limit_bytes=40 * 2**20
        ),
    )(flat(queries), flat(keys), flat(values), flat(attn_grad), flat(attn_out), flat(log_sum), window_dirs)
    return tuple(array.reshape(shape) for array in (dq, dk, dv))


def solution(mesh):
    spec = P("tp", "sh", "sw", None)
    return jax.shard_map(
        functools.partial(local, mesh.shape["sh"], mesh.shape["sw"]),
        mesh=mesh,
        in_specs=(spec,) * 6 + (P(),),
        out_specs=(spec,) * 3,
        check_vma=False,
    )
```

```python
import functools

import jax
import jax.numpy as jnp
from jax import lax
from jax.experimental import pallas as pl
from jax.experimental.pallas import tpu as pltpu
from jax.sharding import PartitionSpec as P

E_OF = (1, 7, 4, 0, 3, 2, 8, 5)
BF = jnp.bfloat16
F32 = jnp.float32
NT = (((1,), (1,)), ((), ()))
TN = (((0,), (0,)), ((), ()))


def kernel(
    n_sh, n_sw, half, hd,
    q_in, k_in, v_in, g_in, o_in, lse_in, wd_in,
    dq_out, dk_out, dv_out,
    zb00, zb01, zb10, zb11, kv0, kv1, qg, pieces, packed, stats,
    q_ref, k_ref, v_ref, g_ref, o_ref, lse_ref, wd_ref, in_sem,
    rs00, rs01, rs02, rs10, rs11, rs12, dqs, dkp, own_kv, own_q,
    zsend, zback, xsend, xback, head_of, rank_of, member_of, flat_of,
    zs, zr, zts, ztr, xs, xr, ws, wr, wts, wtr, rs, rr, rzs, rzr, rxs, rxr,
):
    row = lax.axis_index("sh")
    col = lax.axis_index("sw")
    part = lax.axis_index("tp")
    zb = ((zb00, zb01), (zb10, zb11))
    kv = (kv0, kv1)
    rsw = ((rs00, rs01, rs02), (rs10, rs11, rs12))
    third = half // 2
    tok = q_ref.shape[0]
    arguments = (
        (q_in, q_ref), (g_in, g_ref), (k_in, k_ref), (v_in, v_ref), (wd_in, wd_ref), (o_in, o_ref), (lse_in, lse_ref),
    )
    loads = [pltpu.make_async_copy(src, dst, in_sem.at[i]) for i, (src, dst) in enumerate(arguments)]
    for load in loads:
        load.start()
    scale = hd ** -0.5
    row_ok = lambda step: (row + step >= 0) & (row + step < n_sh)
    col_ok = lambda step: (col + step >= 0) & (col + step < n_sw)
    row_step = (0, -1, 1)
    col_step = (-1, 1)

    def remote(src, dst, ssem, rsem, device):
        return pltpu.make_async_remote_copy(
            src_ref=src, dst_ref=dst, send_sem=ssem, recv_sem=rsem,
            device_id=device, device_id_type=pl.DeviceIdType.MESH,
        )

    def copy_z(run, i):
        return remote(qg.at[run], zb[run][i], zs.at[run, i], zr.at[run, i], {"sh": row + 2 * i - 1})

    def copy_zstat(i):
        return remote(stats.at[6], stats.at[7 + i], zts.at[i], ztr.at[i], {"sh": row + 2 * i - 1})

    def copy_x(run):
        src = kv[run].at[:, :, pl.ds(0, tok)]
        dst = kv[run].at[:, :, pl.ds(tok, tok)]
        return remote(src, dst, xs.at[run], xr.at[run], {"tp": 1 - part})

    def copy_w(run, c, i):
        e = c * 3 + i
        return remote(packed.at[run, e], pieces.at[run, e], ws.at[run, e], wr.at[run, e], {"sw": col + col_step[c]})

    def copy_wstat(c, i):
        e = c * 3 + i
        return remote(stats.at[6 + i], stats.at[e], wts.at[e], wtr.at[e], {"sw": col + col_step[c]})

    def copy_back(run, c, i):
        e = c * 3 + i
        return remote(dqs.at[run * 9 + e], rsw[run][i].at[c], rs.at[run, e], rr.at[run, e], {"sw": col - col_step[c]})

    def copy_zback(run, i):
        return remote(zsend.at[run, i], zback.at[run, i], rzs.at[run, i], rzr.at[run, i], {"sh": row - (2 * i - 1)})

    def copy_xback(run):
        return remote(xsend.at[run], xback.at[run], rxs.at[run], rxr.at[run], {"tp": 1 - part})

    barrier = pltpu.get_barrier_semaphore()
    pl.semaphore_signal(barrier, inc=1, device_id={"tp": 1 - part}, device_id_type=pl.DeviceIdType.MESH)
    for step in (-1, 1):
        @pl.when(row_ok(step))
        def _():
            pl.semaphore_signal(barrier, inc=1, device_id={"sh": row + step}, device_id_type=pl.DeviceIdType.MESH)

        @pl.when(col_ok(step))
        def _():
            pl.semaphore_signal(barrier, inc=1, device_id={"sw": col + step}, device_id_type=pl.DeviceIdType.MESH)
    count = 1
    for step in (-1, 1):
        count = count + row_ok(step).astype(jnp.int32) + col_ok(step).astype(jnp.int32)
    pl.semaphore_wait(barrier, count)

    loads[0].wait()
    loads[1].wait()
    for run in (0, 1):
        for h in range(half):
            cols = slice((run * half + h) * hd, (run * half + h + 1) * hd)
            qg[run, 0, h] = q_ref[:, cols]
            qg[run, 1, h] = g_ref[:, cols]
        for i in (0, 1):
            @pl.when(row_ok(2 * i - 1))
            def _():
                copy_z(run, i).start()
    loads[2].wait()
    loads[3].wait()
    for run in (0, 1):
        for h in range(half):
            cols = slice((run * half + h) * hd, (run * half + h + 1) * hd)
            kv[run][0, h, :tok] = k_ref[:, cols]
            kv[run][1, h, :tok] = v_ref[:, cols]
        copy_x(run).start()

    loads[4].wait()
    for run in (0, 1):
        dirs = [[wd_ref[j, run * half + h] for j in range(4)] for h in range(half)]
        flat = [[jnp.int32(0) for j in range(4)] for h in range(half)]
        for d in range(8):
            e = E_OF[d]
            seen = jnp.int32(0)
            heads = [jnp.int32(0) for _ in range(third)]
            for h in range(half):
                named = [(dirs[h][j] == d).astype(jnp.int32) for j in range(4)]
                member = named[0] + named[1] + named[2] + named[3]
                rank = jnp.minimum(seen, third - 1)
                rank_of[(run * 9 + e) * half + h] = rank
                member_of[(run * 9 + e) * half + h] = member
                at = (run * 9 + e) * third + rank
                for j in range(4):
                    flat[h][j] = flat[h][j] + named[j] * at
                for s in range(third):
                    heads[s] = heads[s] + member * (seen == s).astype(jnp.int32) * h
                seen = seen + member
            for s in range(third):
                head_of[(run * 9 + e) * third + s] = heads[s]
        for h in range(half):
            for j in range(4):
                flat_of[(run * half + h) * 4 + j] = flat[h][j]

    def pack(run, c, i):
        e = c * 3 + i
        for s in range(third):
            h = head_of[(run * 9 + e) * third + s]
            for a in (0, 1):
                block = qg[run, a, h] if i == 0 else zb[run][i - 1][a, h]
                if c == 2:
                    pieces[run, e, s, a] = block
                else:
                    packed[run, e, s, a] = block

    for run in (0, 1):
        for c in (0, 1):
            @pl.when(col_ok(col_step[c]))
            def _():
                pack(run, c, 0)
                copy_w(run, c, 0).start()

    loads[5].wait()
    loads[6].wait()
    lane = lax.broadcasted_iota(jnp.int32, (tok, hd), 1)
    table = jnp.zeros((tok, hd), F32)
    for run in (0, 1):
        for h in range(half):
            at = run * half + h
            cols = slice(at * hd, (at + 1) * hd)
            delta = jnp.sum(g_ref[:, cols].astype(F32) * o_ref[:, cols].astype(F32), axis=1, keepdims=True)
            table = jnp.where(lane == run * 16 + h, lse_ref[:, at:at + 1], table)
            table = jnp.where(lane == run * 16 + 8 + h, delta, table)
    square = jnp.concatenate([table, jnp.zeros((hd - tok, hd), F32)], axis=0) if tok < hd else table
    stats[6] = square.T[:32, :]
    for i in (0, 1):
        @pl.when(row_ok(2 * i - 1))
        def _():
            copy_zstat(i).start()
    for c in (0, 1):
        @pl.when(col_ok(col_step[c]))
        def _():
            copy_wstat(c, 0).start()

    def clear(e, carry):
        i = lax.rem(e, 3)
        c = lax.div(e, 3)
        r_step = jnp.where(i == 0, 0, 2 * i - 3)
        c_step = jnp.where(c == 2, 0, 2 * c - 1)
        live = row_ok(-r_step) & col_ok(-c_step)

        @pl.when(jnp.logical_not(live))
        def _():
            for run in (0, 1):
                for s in range(third):
                    dkp[(run * 9 + e) * third + s] = jnp.zeros(dkp.shape[1:], BF)
        return carry

    lax.fori_loop(0, 9, clear, 0)
    for c in (0, 1):
        @pl.when(jnp.logical_not(col_ok(col_step[c])))
        def _():
            for run in (0, 1):
                for i in range(3):
                    rsw[run][i][c] = jnp.zeros(rs00.shape[1:], BF)
    for i in (0, 1):
        @pl.when(jnp.logical_not(row_ok(2 * i - 1)))
        def _():
            for run in (0, 1):
                zback[run, i] = jnp.zeros(zback.shape[2:], BF)

    sub = lax.broadcasted_iota(jnp.int32, (8, hd), 0)

    def one(run, h, q, g, stat):
        keys = kv[run][0, h]
        vals = kv[run][1, h]
        pick = sub == h
        lse = jnp.sum(jnp.where(pick, stat[run * 16:run * 16 + 8], 0.0), axis=0, keepdims=True)[:, :tok]
        delta = jnp.sum(jnp.where(pick, stat[run * 16 + 8:run * 16 + 16], 0.0), axis=0, keepdims=True)[:, :tok]
        scores = lax.dot_general(keys, q, NT, preferred_element_type=F32)
        prob = jnp.exp(scores * scale - lse)
        grad_prob = lax.dot_general(vals, g, NT, preferred_element_type=F32)
        score_bf = (prob * (grad_prob - delta)).astype(BF)
        prob_bf = prob.astype(BF)
        dv = jnp.dot(prob_bf, g, preferred_element_type=F32)
        dk = jnp.dot(score_bf, q, preferred_element_type=F32) * scale
        dq = lax.dot_general(score_bf, keys, TN, preferred_element_type=F32) * scale
        return dq, dk, dv

    def own(run):
        def body(t, carry):
            stat = stats[6]
            for u in range(3):
                h = t * 3 + u
                dq, dk, dv = one(run, h, qg[run, 0, h], qg[run, 1, h], stat)
                own_q[run * half + h] = dq
                own_kv[run * half + h, 0] = dk
                own_kv[run * half + h, 1] = dv
            return carry

        lax.fori_loop(0, half // 3, body, 0)

    def group(run, e):
        stat = stats[e]
        for s in range(third):
            h = head_of[(run * 9 + e) * third + s]
            dq, dk, dv = one(run, h, pieces[run, e, s, 0], pieces[run, e, s, 1], stat)
            dqs[run * 9 + e, s] = dq.astype(BF)
            dkp[(run * 9 + e) * third + s, 0] = dk.astype(BF)
            dkp[(run * 9 + e) * third + s, 1] = dv.astype(BF)

    def from_side(run, c, i):
        @pl.when(row_ok(-row_step[i]) & col_ok(-col_step[c]))
        def _():
            copy_w(run, c, i).wait_recv()
            if run == 0:
                copy_wstat(c, i).wait_recv()
            group(run, c * 3 + i)
            copy_back(run, c, i).start()

    def relay(run):
        for i in (1, 2):
            @pl.when(row_ok(-row_step[i]))
            def _():
                copy_z(run, i - 1).wait_recv()
                if run == 0:
                    copy_zstat(i - 1).wait_recv()
                for c in (0, 1):
                    @pl.when(col_ok(col_step[c]))
                    def _():
                        pack(run, c, i)
                        copy_w(run, c, i).start()
                        if run == 0:
                            copy_wstat(c, i).start()
                pack(run, 2, i)

    def from_rows(run):
        for i in (1, 2):
            @pl.when(row_ok(-row_step[i]))
            def _():
                group(run, 6 + i)

    def wait_back(run, i):
        for c in (0, 1):
            @pl.when(row_ok(-row_step[i]) & col_ok(col_step[c]))
            def _():
                copy_back(run, c, i).wait_recv()

    def gathered(run, i, h, total):
        for c in (0, 1, 2):
            if c == 2 and i == 0:
                continue
            e = c * 3 + i
            rank = rank_of[(run * 9 + e) * half + h]
            held = dqs[run * 9 + e, rank] if c == 2 else rsw[run][i][c, rank]
            block = held.astype(F32) * member_of[(run * 9 + e) * half + h].astype(F32)
            total = block if total is None else total + block
        return total

    def turn(run):
        for i in (1, 2):
            @pl.when(row_ok(-row_step[i]))
            def _():
                wait_back(run, i)

                def body(h, carry):
                    zsend[run, i - 1, h] = gathered(run, i, h, None).astype(BF)
                    return carry

                lax.fori_loop(0, half, body, 0)
                copy_zback(run, i - 1).start()

    def total_kv(run, h, rows, a):
        total = own_kv[run * half + h, a, rows]
        for j in range(4):
            at = flat_of[(run * half + h) * 4 + j]
            total = total + dkp[at, a, rows].astype(F32)
        return total

    def to_partner(run):
        def body(h, carry):
            for a in (0, 1):
                xsend[run, a, h] = total_kv(run, h, slice(tok, 2 * tok), a).astype(BF)
            return carry

        lax.fori_loop(0, half, body, 0)
        copy_xback(run).start()

    def finish_kv(run):
        copy_xback(run).wait_recv()

        def body(h, carry):
            cols = pl.ds(pl.multiple_of((run * half + h) * hd, hd), hd)
            for a, out in ((0, dk_out), (1, dv_out)):
                total = total_kv(run, h, slice(0, tok), a) + xback[run, a, h].astype(F32)
                out[:, cols] = total.astype(BF)
            return carry

        lax.fori_loop(0, half, body, 0)

    def finish_q(run):
        wait_back(run, 0)
        for i in (0, 1):
            @pl.when(row_ok(2 * i - 1))
            def _():
                copy_zback(run, i).wait_recv()

        def body(h, carry):
            cols = pl.ds(pl.multiple_of((run * half + h) * hd, hd), hd)
            total = gathered(run, 0, h, own_q[run * half + h])
            total = total + zback[run, 0, h].astype(F32) + zback[run, 1, h].astype(F32)
            dq_out[:, cols] = total.astype(BF)
            return carry

        lax.fori_loop(0, half, body, 0)

    relay(0)
    copy_x(0).wait_recv()
    own(0)
    from_side(0, 0, 0)
    from_side(0, 1, 0)
    relay(1)
    from_rows(0)
    for i in (1, 2):
        for c in (0, 1):
            from_side(0, c, i)
    to_partner(0)
    copy_x(1).wait_recv()
    from_rows(1)
    turn(0)
    for i in (1, 2):
        for c in (0, 1):
            from_side(1, c, i)
    from_side(1, 0, 0)
    from_side(1, 1, 0)
    own(1)
    to_partner(1)
    turn(1)
    finish_kv(0)
    finish_q(0)
    finish_kv(1)
    finish_q(1)

    for run in (0, 1):
        copy_x(run).wait_send()
        copy_xback(run).wait_send()
        for i in (0, 1):
            @pl.when(row_ok(2 * i - 1))
            def _():
                copy_z(run, i).wait_send()
                if run == 0:
                    copy_zstat(i).wait_send()

            @pl.when(row_ok(1 - 2 * i))
            def _():
                copy_zback(run, i).wait_send()
        for c in (0, 1):
            for i in range(3):
                @pl.when(row_ok(-row_step[i]) & col_ok(col_step[c]))
                def _():
                    copy_w(run, c, i).wait_send()
                    if run == 0:
                        copy_wstat(c, i).wait_send()

                @pl.when(row_ok(-row_step[i]) & col_ok(-col_step[c]))
                def _():
                    copy_back(run, c, i).wait_send()


def hand_out(a_in, b_in, c_in, a_out, b_out, c_out, held, in_sem, out_sem):
    ins = [pltpu.make_async_copy(src, held.at[i], in_sem.at[i]) for i, src in enumerate((a_in, b_in, c_in))]
    outs = [pltpu.make_async_copy(held.at[i], dst, out_sem.at[i]) for i, dst in enumerate((a_out, b_out, c_out))]
    for copy in ins:
        copy.start()
    for first, second in zip(ins, outs):
        first.wait()
        second.start()
    for copy in outs:
        copy.wait()


def local(n_sh, n_sw, queries, keys, values, attn_out, attn_grad, log_sum, window_dirs):
    shape = queries.shape
    tok = shape[0] * shape[1] * shape[2]
    cols = shape[3]
    heads = log_sum.shape[3]
    half = heads // 2
    third = half // 2
    hd = cols // heads
    flat = lambda array: array.reshape(tok, array.shape[3])
    vmem = pl.BlockSpec(memory_space=pltpu.VMEM)
    hbm = pl.BlockSpec(memory_space=pltpu.HBM)
    dma = pltpu.SemaphoreType.DMA
    scratch = (
        [pltpu.VMEM((2, half, tok, hd), BF) for _ in range(4)]
        + [pltpu.VMEM((2, half, 2 * tok, hd), BF) for _ in range(2)]
        + [
            pltpu.VMEM((2, 2, half, tok, hd), BF),
            pltpu.VMEM((2, 9, third, 2, tok, hd), BF),
            pltpu.VMEM((2, 6, third, 2, tok, hd), BF),
            pltpu.VMEM((9, 32, hd), F32),
        ]
        + [pltpu.VMEM((tok, cols), BF) for _ in range(5)]
        + [pltpu.VMEM((tok, heads), F32), pltpu.SMEM((4, heads), jnp.int32), dma((7,))]
        + [pltpu.VMEM((2, third, tok, hd), BF) for _ in range(6)]
        + [
            pltpu.VMEM((18, third, tok, hd), BF),
            pltpu.VMEM((18 * third, 2, 2 * tok, hd), BF),
            pltpu.VMEM((heads, 2, 2 * tok, hd), F32),
            pltpu.VMEM((heads, tok, hd), F32),
            pltpu.VMEM((2, 2, half, tok, hd), BF),
            pltpu.VMEM((2, 2, half, tok, hd), BF),
            pltpu.VMEM((2, 2, half, tok, hd), BF),
            pltpu.VMEM((2, 2, half, tok, hd), BF),
            pltpu.SMEM((18 * third,), jnp.int32),
            pltpu.SMEM((18 * half,), jnp.int32),
            pltpu.SMEM((18 * half,), jnp.int32),
            pltpu.SMEM((heads * 4,), jnp.int32),
        ]
    )
    for sem in ((2, 2), (2,), (2,), (2, 6), (6,), (2, 6), (2, 2), (2,)):
        scratch += [dma(sem), dma(sem)]
    dq, dk, dv = pl.pallas_call(
        functools.partial(kernel, n_sh, n_sw, half, hd),
        out_shape=[jax.ShapeDtypeStruct((tok, cols), BF)] * 3,
        in_specs=[hbm] * 7,
        out_specs=[vmem] * 3,
        scratch_shapes=scratch,
        compiler_params=pltpu.CompilerParams(
            collective_id=0, has_side_effects=True, vmem_limit_bytes=64 * 2**20
        ),
    )(flat(queries), flat(keys), flat(values), flat(attn_grad), flat(attn_out), flat(log_sum), window_dirs.T)
    dq, dk, dv = pl.pallas_call(
        hand_out,
        out_shape=[jax.ShapeDtypeStruct((tok, cols), BF)] * 3,
        in_specs=[hbm] * 3,
        out_specs=[hbm] * 3,
        scratch_shapes=[pltpu.VMEM((3, tok, cols), BF), dma((3,)), dma((3,))],
        compiler_params=pltpu.CompilerParams(vmem_limit_bytes=64 * 2**20),
    )(dq, dk, dv)
    return tuple(array.reshape(shape) for array in (dq, dk, dv))


def solution(mesh):
    spec = P("tp", "sh", "sw", None)
    return jax.shard_map(
        functools.partial(local, mesh.shape["sh"], mesh.shape["sw"]),
        mesh=mesh,
        in_specs=(spec,) * 6 + (P(),),
        out_specs=(spec,) * 3,
        check_vma=False,
    )
```
